128 devices in a mesh: rep: 2 (over x_hi), shard: 64 (over z, x_lo, y, core).
Axes of the slice: x: 4 (x_hi: 2, x_lo: 2; x = x_hi * 2 + x_lo), y: 4, z: 4, core: 2. Of those that a mesh axis runs over, the one named last changes fastest.
Arguments:
- tokens: bfloat16 [16384, 2048], P(('rep', 'shard')), may hold values from -6 to 6
- cotangent: bfloat16 [16384, 2048], P(('rep', 'shard')), may hold values from -6 to 6
- segments: int32 [128, 128], P(('rep', 'shard')), may hold values from 0 to 15, never falling along the last dimension, each value on 1 to 64 neighbouring positions
- project_in: float32 [2048, 3072], P('shard'), may hold values from -0.125 to 0.125
- project_out: float32 [2048, 2048], P('shard'), may hold values from -0.5 to 0.5
- gate_up: float32 [2, 2048, 8192], P(None, None, 'shard'), may hold values from -0.125 to 0.125
- down_weight: float32 [8192, 2048], P('shard'), may hold values from -0.125 to 0.125
- norm_gains: float32 [2, 2048], P(None, 'shard'), may hold values from 0.1 to 1.9
- first_in: float32 [2048, 3072], P('shard'), may hold values from -80 to 80
- first_out: float32 [2048, 2048], P('shard'), may hold values from -80 to 80
- first_gate: float32 [2, 2048, 8192], P(None, None, 'shard'), may hold values from -80 to 80
- first_down: float32 [8192, 2048], P('shard'), may hold values from -80 to 80
- first_gains: float32 [2, 2048], P(None, 'shard'), may hold values from -256 to 256
- second_in: float32 [2048, 3072], P('shard'), may hold values from 901.12 to 3604.48
- second_out: float32 [2048, 2048], P('shard'), may hold values from 901.12 to 3604.48
- second_gate: float32 [2, 2048, 8192], P(None, None, 'shard'), may hold values from 901.12 to 3604.48
- second_down: float32 [8192, 2048], P('shard'), may hold values from 901.12 to 3604.48
- second_gains: float32 [2, 2048], P(None, 'shard'), may hold values from 8192 to 32768
Outputs:
- layer_out: float32 [16384, 2048], P(('rep', 'shard'))
- input_grad: float32 [16384, 2048], P(('rep', 'shard'))
- new_in: float32 [2048, 3072], P('shard')
- new_out: float32 [2048, 2048], P('shard')
- new_gate: float32 [2, 2048, 8192], P(None, None, 'shard')
- new_down: float32 [8192, 2048], P('shard')
- new_gains: float32 [2, 2048], P(None, 'shard')
- moment_in: float32 [2048, 3072], P('shard')
- moment_out: float32 [2048, 2048], P('shard')
- moment_gate: float32 [2, 2048, 8192], P(None, None, 'shard')
- moment_down: float32 [8192, 2048], P('shard')
- moment_gains: float32 [2, 2048], P(None, 'shard')
- square_in: float32 [2048, 3072], P('shard')
- square_out: float32 [2048, 2048], P('shard')
- square_gate: float32 [2, 2048, 8192], P(None, None, 'shard')
- square_down: float32 [8192, 2048], P('shard')
- square_gains: float32 [2, 2048], P(None, 'shard')
The draws below stay inside these ranges and needn't reach their ends.
Inputs may be any that keep to these rules, and one draw needn't show every extreme that they name: `segments`: within each sequence the document numbers never fall and start at 0; every document holds 1 to 64 tokens, and one of each sequence holds exactly 64.
All inputs are finite; a program needn't handle non-finite values.
Results may differ from the reference program's by a relative error of at most 0.02.
Values may be sent and summed in bfloat16 or wider, within the bound.
No kernel may reach another device: no remote copies, remote signals or barrier semaphores. Data moves between devices by JAX's collectives and lax.ppermute only.
A program may use at most 576 MiB of HBM per device.

```python
import math
import jax
import jax.numpy as jnp
import numpy as np
from jax import lax

D = 2048
HEADS = 32
KV_HEADS = 8
HEAD_DIM = 64
FF = 8192
SEQ = 128
STEP = 10
QKV = 3072
NSEQ = 128
TOKENS = 16384


def steps_of(key, dims, shards, smallest, high):
    loudness, own = 1.0, jax.random.fold_in(key, 6)
    for axis_at, blocks in shards:
        steps = jnp.exp(jax.random.uniform(jax.random.fold_in(own, axis_at), (blocks,), jnp.float32, smallest / len(shards), high / len(shards)))
        loudness = loudness * jnp.repeat(steps, dims[axis_at] // blocks).reshape([-1 if axis == axis_at else 1 for axis in range(len(dims))])
    return loudness


def split_up(number_of, total, reach, lean):
    weights = [(1 << 20) // math.isqrt(grade ** lean) + 1 for grade in range(2, number_of + 1)]
    surplus, holding = total - reach - (number_of - 1), [1] * (number_of - 1)
    while surplus > 0:
        free = [i for i in range(number_of - 1) if holding[i] < reach]
        pool, budget = sum([weights[i] for i in free]), surplus
        for i in free:
            extra = min(reach - holding[i], max(1, budget * weights[i] // pool), surplus)
            holding[i] = holding[i] + extra
            surplus = surplus - extra
    return np.array([reach] + holding)


def ragged_sizes(key, amount, total, limit, skew):
    if amount == 2:
        one = jax.random.randint(key, (), max(1, total - limit), min(limit, total - 1) + 1)
        return jnp.stack([one, total - one])
    tallies = jnp.asarray(split_up(amount, total, limit, skew), jnp.int32)
    pairs = (amount - 1) // 2
    giver, sink = tallies[1:1 + 2 * pairs:2], tallies[2:2 + 2 * pairs:2]
    margin = jnp.minimum(giver - 1, limit - sink)
    shifted = jax.random.randint(jax.random.fold_in(key, 1), (pairs,), 0, 1 << 20) % (margin + 1)
    tallies = tallies.at[1:1 + 2 * pairs:2].set(giver - shifted).at[2:2 + 2 * pairs:2].set(sink + shifted)
    return tallies[jax.random.permutation(jax.random.fold_in(key, 2), amount)]


def normal_values(stream_key, extent, width, limit, split=(), kind=jnp.bfloat16):
    array = jax.random.normal(stream_key, extent, jnp.float32) * width
    if len(split) > 0:
        array = steps_of(stream_key, extent, split, -0.22, 0.18) * array
    return jnp.clip(array, min=-limit, max=limit).astype(kind)


def setup_inputs(seed: int = 0) -> dict:
    seeds = jax.random.split(jax.random.key(seed), 19)
    return {
        "tokens": normal_values(seeds[0], (TOKENS, D), 1.0, 6.0, ((0, 128),)),
        "cotangent": normal_values(seeds[1], (TOKENS, D), 1.0, 6.0, ((0, 128),)),
        "segments": jax.vmap(lambda own: jnp.searchsorted(jnp.cumsum(ragged_sizes(own, SEQ // 8, SEQ, SEQ // 2, 2)), jnp.arange(SEQ), side="right"))(jax.random.split(seeds[2], NSEQ)).reshape((NSEQ, SEQ)).astype(jnp.int32),
        "project_in": normal_values(seeds[3], (D, QKV), D ** -0.5, 0.125, ((0, 64),), jnp.float32),
        "project_out": normal_values(seeds[4], (HEADS * HEAD_DIM, D), (D // 16) ** -0.5, 0.5, ((0, 64),), jnp.float32),
        "gate_up": normal_values(seeds[5], (2, D, FF), D ** -0.5, 0.125, ((2, 64),), jnp.float32),
        "down_weight": normal_values(seeds[6], (FF, D), (FF // 4) ** -0.5, 0.125, ((0, 64),), jnp.float32),
        "norm_gains": jnp.clip(1.0 + 0.18 * jax.random.normal(seeds[7], (2, D), jnp.float32), 0.1, 1.9),
        "first_in": normal_values(seeds[8], (D, QKV), (0.11 * TOKENS ** 0.5), 80.0, ((0, 64),), jnp.float32),
        "first_out": normal_values(seeds[9], (HEADS * HEAD_DIM, D), (0.11 * TOKENS ** 0.5), 80.0, ((0, 64),), jnp.float32),
        "first_gate": normal_values(seeds[10], (2, D, FF), (0.11 * TOKENS ** 0.5), 80.0, ((2, 64),), jnp.float32),
        "first_down": normal_values(seeds[11], (FF, D), (0.11 * TOKENS ** 0.5), 80.0, ((0, 64),), jnp.float32),
        "first_gains": normal_values(seeds[12], (2, D), (0.33 * TOKENS ** 0.5), 256.0, ((1, 64),), jnp.float32),
        "second_in": jnp.clip(jnp.exp(math.log(3604.48) - 1.3862944 * jax.random.uniform(seeds[13], (D, QKV), jnp.float32) ** steps_of(seeds[13], (D, QKV), ((0, 64),), -0.2, 0.2)), 901.12, 3604.48),
        "second_out": jnp.clip(jnp.exp(math.log(3604.48) - 1.3862944 * jax.random.uniform(seeds[14], (HEADS * HEAD_DIM, D), jnp.float32) ** steps_of(seeds[14], (HEADS * HEAD_DIM, D), ((0, 64),), -0.2, 0.2)), 901.12, 3604.48),
        "second_gate": jnp.clip(jnp.exp(math.log(3604.48) - 1.3862944 * jax.random.uniform(seeds[15], (2, D, FF), jnp.float32) ** steps_of(seeds[15], (2, D, FF), ((2, 64),), -0.2, 0.2)), 901.12, 3604.48),
        "second_down": jnp.clip(jnp.exp(math.log(3604.48) - 1.3862944 * jax.random.uniform(seeds[16], (FF, D), jnp.float32) ** steps_of(seeds[16], (FF, D), ((0, 64),), -0.2, 0.2)), 901.12, 3604.48),
        "second_gains": jnp.clip(jnp.exp(math.log(32768.0) - 1.3862944 * jax.random.uniform(seeds[17], (2, D), jnp.float32) ** steps_of(seeds[17], (2, D), ((1, 64),), -0.2, 0.2)), 8192.0, 32768.0),
    }


@jax.custom_vjp
def low(v):
    return lax.optimization_barrier(v.astype(jnp.bfloat16)).astype(jnp.float32)

@jax.custom_vjp
def low_back(v):
    return v

def low_keep(v):
    return (low(v), None)

def low_pass(kept, grad):
    return (grad,)

def back_keep(v):
    return (v, None)

def back_low(kept, grad):
    return (low(grad),)
low.defvjp(low_keep, low_pass)
low_back.defvjp(back_keep, back_low)
eps_norm = 1e-05
rope_base = 500000.0
beta_one = 0.9
beta_two = 0.95
adam_eps = 1e-08
rate_matrix = 0.1
rate_gain = 1.0
decay_matrix = 0.1

def positions_of(segments):
    seq_len = segments.shape[-1]
    token_index = jnp.arange(seq_len, dtype=jnp.int32)
    changes = jnp.concatenate([jnp.ones_like(segments[..., :1]), (segments[..., 1:] != segments[..., :-1]).astype(jnp.int32)], axis=-1)
    starts = jnp.where(changes > 0, token_index, 0).astype(jnp.int32)
    return token_index - lax.cummax(starts, axis=segments.ndim - 1)

def rotate(vectors, position, turn_sign):
    half_dim = vectors.shape[-1] // 2
    frequency = rope_base ** (-jnp.arange(half_dim, dtype=jnp.float32) * 2.0 / vectors.shape[-1])
    angles = position.astype(jnp.float32)[..., None] * frequency
    cosine = jnp.cos(angles)[..., None, :]
    sine_part = turn_sign * jnp.sin(angles)[..., None, :]
    first_half = vectors[..., :half_dim]
    second_half = vectors[..., half_dim:]
    return jnp.concatenate([first_half * cosine - second_half * sine_part, second_half * cosine + first_half * sine_part], axis=-1)

def block_forward(inputs, project_in, project_out, gate_up, down_weight, norm_gains, allowed, position):
    highest = lax.Precision.HIGHEST
    batch_size, seq_len, model_width = inputs.shape
    query_width = HEADS * HEAD_DIM
    kv_width = KV_HEADS * HEAD_DIM
    group_size = HEADS // KV_HEADS
    gains_low = low(norm_gains)
    unit_one = inputs * lax.rsqrt(lax.optimization_barrier(jnp.mean(inputs * inputs, axis=-1, keepdims=True)) + eps_norm)
    normed_one = low(unit_one * gains_low[0])
    mixed_in = low_back(jnp.einsum('bsd,de->bse', normed_one, low(project_in), precision=highest))
    query_raw = mixed_in[..., :query_width].reshape(batch_size, seq_len, HEADS, HEAD_DIM)
    key_raw = mixed_in[..., query_width:query_width + kv_width].reshape(batch_size, seq_len, KV_HEADS, HEAD_DIM)
    value_raw = mixed_in[..., query_width + kv_width:].reshape(batch_size, seq_len, KV_HEADS, HEAD_DIM)
    queries = low(rotate(query_raw, position, 1.0)).reshape(batch_size, seq_len, KV_HEADS, group_size, HEAD_DIM)
    key_rows = low(rotate(key_raw, position, 1.0))
    values = low(value_raw)
    scores = jnp.einsum('bakgd,bckd->bkgac', queries, key_rows, precision=highest) * HEAD_DIM ** (-0.5)
    scores = low_back(jnp.where(allowed[:, None, None], scores, -1e+30))
    soft_probs = low(jax.nn.softmax(scores, axis=-1))
    attended = jnp.einsum('bkgac,bckd->bakgd', soft_probs, values, precision=highest).reshape(batch_size, seq_len, query_width)
    attended = low(low_back(attended))
    hidden = inputs + low_back(jnp.einsum('bse,ed->bsd', attended, low(project_out), precision=highest))
    unit_two = hidden * lax.rsqrt(lax.optimization_barrier(jnp.mean(hidden * hidden, axis=-1, keepdims=True)) + eps_norm)
    normed_two = low(unit_two * gains_low[1])
    gate_pre = low_back(jnp.einsum('bsd,df->bsf', normed_two, low(gate_up[0]), precision=highest))
    up_pre = low_back(jnp.einsum('bsd,df->bsf', normed_two, low(gate_up[1]), precision=highest))
    activated = low(jax.nn.silu(gate_pre) * up_pre)
    return hidden + low_back(jnp.einsum('bsf,fd->bsd', activated, low(down_weight), precision=highest))

def adam_update(master, gradient, moment_old, square_old, step_rate, decay_rate):
    moment_new = beta_one * moment_old + (1.0 - beta_one) * gradient
    square_new = beta_two * square_old + (1.0 - beta_two) * gradient * gradient
    moment_hat = moment_new / (1.0 - beta_one ** STEP)
    square_hat = square_new / (1.0 - beta_two ** STEP)
    updated = master - step_rate * (moment_hat / (jnp.sqrt(square_hat) + adam_eps) + decay_rate * master)
    return (updated, moment_new, square_new)

def reference(tokens, cotangent, segments, project_in, project_out, gate_up, down_weight, norm_gains, first_in, first_out, first_gate, first_down, first_gains, second_in, second_out, second_gate, second_down, second_gains):
    group_count = math.gcd(NSEQ, max(1, 4096 // SEQ))
    block_count = NSEQ // group_count
    inputs = tokens.astype(jnp.float32).reshape(block_count, group_count, SEQ, D)
    grad_out = cotangent.astype(jnp.float32).reshape(block_count, group_count, SEQ, D)
    seg_blocks = segments.reshape(block_count, group_count, SEQ)
    params = (project_in, project_out, gate_up, down_weight, norm_gains)
    token_index = jnp.arange(SEQ, dtype=jnp.int32)
    causal = token_index[:, None] >= token_index[None, :]

    def block_step(totals, block_in):
        block_values, block_grad, block_seg = block_in
        position = positions_of(block_seg)
        allowed = (block_seg[:, :, None] == block_seg[:, None, :]) & causal[None]

        def forward(values_in, *weights):
            return block_forward(values_in, *weights, allowed, position)
        output, pullback = jax.vjp(forward, block_values, *params)
        gradients = pullback(block_grad)
        summed = tuple((total + grad_part for total, grad_part in zip(totals, gradients[1:])))
        return (summed, (output, gradients[0]))
    zero_sums = tuple((jnp.zeros_like(weight_part) for weight_part in params))
    totals, (outputs, input_grads) = lax.scan(block_step, zero_sums, (inputs, grad_out, seg_blocks))
    grad_in, grad_out_proj, grad_gate, grad_down, grad_gains = totals
    new_in, moment_in, square_in = adam_update(project_in, grad_in, first_in, second_in, rate_matrix, decay_matrix)
    new_out, moment_out, square_out = adam_update(project_out, grad_out_proj, first_out, second_out, rate_matrix, decay_matrix)
    new_gate, moment_gate, square_gate = adam_update(gate_up, grad_gate, first_gate, second_gate, rate_matrix, decay_matrix)
    new_down, moment_down, square_down = adam_update(down_weight, grad_down, first_down, second_down, rate_matrix, decay_matrix)
    new_gains, moment_gains, square_gains = adam_update(norm_gains, grad_gains, first_gains, second_gains, rate_gain, 0.0)
    layer_out = outputs.reshape(TOKENS, D)
    input_grad = input_grads.reshape(TOKENS, D)
    return (layer_out, input_grad, new_in, new_out, new_gate, new_down, new_gains, moment_in, moment_out, moment_gate, moment_down, moment_gains, square_in, square_out, square_gate, square_down, square_gains)
```

```python
import jax
import jax.numpy as jnp
from jax import lax
from jax.sharding import PartitionSpec as P

HEADS = 32
KV_HEADS = 8
HEAD_DIM = 64
STEP = 10
GROUP = HEADS // KV_HEADS
EVERY = ("rep", "shard")

eps_norm = 1e-05
rope_base = 500000.0
beta_one = 0.9
beta_two = 0.95
adam_eps = 1e-08
rate_matrix = 0.1
rate_gain = 1.0
decay_matrix = 0.1

low_type = jnp.bfloat16
f32 = jnp.float32


def pairs_of(move):
    pairs = []
    for device in range(128):
        c, y, x = device % 2, device // 2 % 4, device // 8 % 2
        z, rep = device // 16 % 4, device // 64
        rep, z, x, y, c = move(rep, z, x, y, c)
        pairs.append((device, rep * 64 + ((z * 2 + x) * 4 + y) * 2 + c))
    return pairs


def x_moved(rep, x, by):
    at = (rep * 2 + x + by) % 4
    return at // 2, at % 2


def go_y(by):
    return pairs_of(lambda rep, z, x, y, c: (rep, z, x, (y + by) % 4, c))


def go_z(by):
    return pairs_of(lambda rep, z, x, y, c: (rep, (z + by) % 4, x, y, c))


def go_x(by):
    def move(rep, z, x, y, c):
        rep, x = x_moved(rep, x, by)
        return rep, z, x, y, c

    return pairs_of(move)


go_core = pairs_of(lambda rep, z, x, y, c: (rep, z, x, y, 1 - c))
go_rep = pairs_of(lambda rep, z, x, y, c: (1 - rep, z, x, y, c))
go_turn = pairs_of(lambda rep, z, x, y, c: (rep, y, c, z, x))


def send(value, pairs):
    return lax.ppermute(value, EVERY, pairs)


def ring_gather(own, step):
    half = own.shape[0] // 2
    left = send(own, step(1))
    right = send(own, step(-1))
    across = jnp.concatenate([send(left[:half], step(1)), send(right[half:], step(-1))])
    return own, left, right, across


def ring_reduce(own, left, right, across, step):
    half = own.shape[0] // 2
    to_right = send(across[:half], step(1))
    to_left = send(across[half:], step(-1))
    right = jnp.concatenate([added(right[:half], to_right), right[half:]])
    left = jnp.concatenate([left[:half], added(left[half:], to_left)])
    got_left = send(right, step(1))
    got_right = send(left, step(-1))
    return own.astype(f32) + got_left.astype(f32) + got_right.astype(f32)


def added(one, two):
    return (one.astype(f32) + two.astype(f32)).astype(low_type)


token_groups = [[f * 8 + t for t in range(8)] for f in range(8)]
y_groups = [[f * 8 + y * 2 + c for y in range(4)] for f in range(8) for c in range(2)]
z_groups = [[z * 16 + x * 8 + t for z in range(4)] for x in range(2) for t in range(8)]


def swap(parts, groups):
    return lax.all_to_all(parts, "shard", 0, 0, axis_index_groups=groups, tiled=True)


def gather(own, groups):
    return swap(jnp.broadcast_to(own[None], (len(groups[0]),) + own.shape), groups)


def gather_tokens(own):
    mine = gather(own, y_groups)
    return mine, jnp.concatenate([mine, send(mine, go_core)])


def reduce_tokens(parts):
    half = parts.shape[0] // 2
    mine = added(parts[:half], send(parts[half:], go_core))
    return swap(mine.reshape((4, -1) + mine.shape[1:]), y_groups).astype(f32).sum(axis=0)


def mate_along_x(own):
    half = own.shape[0] // 2
    return jnp.concatenate([send(own[:half], go_x(1)), send(own[half:], go_x(-1))])


def gather_weights(own):
    own, left, right, across = ring_gather(own, go_z)
    others = [send(left, go_x(1)), send(right, go_x(-1))]
    return [own, left, right, across, mate_along_x(own)] + others + [mate_along_x(across)]


def reduce_weights(blocks):
    across = added(blocks[3], mate_along_x(blocks[7]))
    left = added(blocks[1], send(blocks[5], go_x(-1)))
    right = added(blocks[2], send(blocks[6], go_x(1)))
    own = added(blocks[0], mate_along_x(blocks[4]))
    return ring_reduce(own, left, right, across, go_z)


def sum_replicas(part):
    return part.astype(f32) + send(part.astype(low_type), go_rep).astype(f32)


def gather_small(own, x):
    column = gather(own, z_groups)
    other = mate_along_x(column)
    both = jnp.stack([jnp.where(x == 0, column, other), jnp.where(x == 0, other, column)], axis=1)
    return both.reshape((8,) + own.shape)


def reduce_small(parts, x):
    column = swap(parts.reshape((4, 2) + parts.shape[1:]), z_groups)
    column = column.astype(f32).sum(axis=0).astype(low_type)
    mine = lax.dynamic_index_in_dim(column, x, 0, keepdims=False)
    mates = lax.dynamic_index_in_dim(column, 1 - x, 0, keepdims=False)
    total = mine.astype(f32) + send(mates, go_x(1)).astype(f32)
    return total + send(mates, go_x(-1)).astype(f32) + send(mine, go_rep).astype(f32)


def after(value, *earlier):
    return lax.optimization_barrier((value,) + earlier)[0]


def positions_of(segments):
    seq_len = segments.shape[-1]
    token_index = jnp.arange(seq_len, dtype=jnp.int32)
    changes = jnp.concatenate(
        [
            jnp.ones_like(segments[..., :1]),
            (segments[..., 1:] != segments[..., :-1]).astype(jnp.int32),
        ],
        axis=-1,
    )
    starts = jnp.where(changes > 0, token_index, 0)
    return token_index - lax.cummax(starts, axis=segments.ndim - 1)


def rotate(vectors, cosine, sine):
    half_dim = vectors.shape[-1] // 2
    first_half = vectors[..., :half_dim]
    second_half = vectors[..., half_dim:]
    return jnp.concatenate(
        [
            first_half * cosine - second_half * sine,
            second_half * cosine + first_half * sine,
        ],
        axis=-1,
    )


def normalize(values):
    inverse = lax.rsqrt(jnp.mean(values * values, axis=-1, keepdims=True) + eps_norm)
    return (values * inverse, inverse)


def norm_back(grad_unit, unit_rows, inverse):
    return inverse * (
        grad_unit - unit_rows * jnp.mean(grad_unit * unit_rows, axis=-1, keepdims=True)
    )


def adam_update(master, gradient, moment_old, square_old, step_rate, decay_rate):
    moment_new = beta_one * moment_old + (1.0 - beta_one) * gradient
    square_new = beta_two * square_old + (1.0 - beta_two) * gradient * gradient
    moment_hat = moment_new / (1.0 - beta_one**STEP)
    square_hat = square_new / (1.0 - beta_two**STEP)
    updated = master - step_rate * (
        moment_hat / (jnp.sqrt(square_hat) + adam_eps) + decay_rate * master
    )
    return (updated, moment_new, square_new)


def dot(left_rows, right_rows):
    return jnp.dot(left_rows, right_rows, preferred_element_type=f32)


def left_dot(left_rows, right_rows):
    return lax.dot_general(
        left_rows, right_rows, (((0,), (0,)), ((), ())), preferred_element_type=f32
    )


def right_dot(left_rows, right_rows):
    return lax.dot_general(
        left_rows, right_rows, (((1,), (1,)), ((), ())), preferred_element_type=f32
    )


def masked_scores(queries, key_rows, allowed):
    scores = jnp.einsum("sagd,scd->sgac", queries, key_rows, preferred_element_type=f32)
    return jnp.where(allowed[:, None], scores * HEAD_DIM ** (-0.5), -1e30)


def local(
    tokens,
    cotangent,
    segments,
    project_in,
    project_out,
    gate_up,
    down_weight,
    norm_gains,
    first_in,
    first_out,
    first_gate,
    first_down,
    first_gains,
    second_in,
    second_out,
    second_gate,
    second_down,
    second_gains,
):
    place = lax.axis_index("shard")
    c, x = place % 2, place // 8 % 2
    seq_len, width = tokens.shape
    inputs = tokens.astype(f32)
    grad_out = cotangent.astype(f32)

    gains_low = norm_gains.astype(low_type)
    gain_rows = gains_low[0].astype(f32)[:, None]
    low_in = project_in.astype(low_type).astype(f32)
    folded = (low_in * gain_rows).astype(low_type)
    query_width, kv_width = HEADS * HEAD_DIM, KV_HEADS * HEAD_DIM
    own_rows = folded.shape[0]
    by_group = jnp.concatenate(
        [
            folded[:, :query_width].reshape(own_rows, KV_HEADS, GROUP * HEAD_DIM),
            folded[:, query_width : query_width + kv_width].reshape(own_rows, KV_HEADS, HEAD_DIM),
            folded[:, query_width + kv_width :].reshape(own_rows, KV_HEADS, HEAD_DIM),
        ],
        axis=2,
    )
    group_width = by_group.shape[2]
    by_source = swap(by_group.transpose(1, 0, 2), token_groups)
    head_in = gather_small(by_source.reshape(8 * own_rows, group_width), x)
    head_in = head_in.reshape(-1, group_width)

    own_gu = jnp.concatenate([gate_up[0].astype(low_type).T, gate_up[1].astype(low_type).T])
    units_own = down_weight.shape[0]
    blocks = gather_weights(jnp.concatenate([own_gu, down_weight.astype(low_type)]))

    seg_all = gather(segments, token_groups).reshape(4, 2, seq_len)
    seg_all = jnp.concatenate(
        [lax.dynamic_index_in_dim(seg_all, core, 1, keepdims=False) for core in (c, 1 - c)]
    )
    position = positions_of(seg_all)
    token_index = jnp.arange(seq_len, dtype=jnp.int32)
    allowed = (seg_all[:, :, None] == seg_all[:, None, :]) & (
        token_index[None, :, None] >= token_index[None, None, :]
    )
    frequency = rope_base ** (-jnp.arange(HEAD_DIM // 2, dtype=f32) * 2.0 / HEAD_DIM)
    angles = position.astype(f32)[..., None] * frequency
    cosine, sine = jnp.cos(angles)[:, :, None], jnp.sin(angles)[:, :, None]

    unit_one, inverse_one = normalize(inputs)
    some_units, units_one = gather_tokens(after(unit_one.astype(low_type), head_in))
    units_one = after(units_one.reshape(-1, width), blocks[1], blocks[2])

    gain_tile = jnp.pad(gains_low[1:], ((0, 15), (0, width - own_rows)))
    out_tile = jnp.concatenate([project_out.astype(low_type), gain_tile])
    out_tiles = gather_small(after(send(out_tile, go_turn), some_units), x)
    head_out = out_tiles[:, :own_rows].reshape(-1, width)
    gain_two = gather(out_tiles[:, own_rows, :own_rows].reshape(1, -1), token_groups)
    gain_two = gain_two.reshape(width).astype(f32)
    cots = gather_tokens(after(cotangent, out_tiles))[1].reshape(-1, width)
    mixed = dot(units_one, head_in).reshape(8, seq_len, group_width)
    q_width = GROUP * HEAD_DIM
    queries = rotate(mixed[..., :q_width].reshape(8, seq_len, GROUP, HEAD_DIM), cosine, sine)
    queries = queries.astype(low_type)
    key_rows = rotate(mixed[..., None, q_width : q_width + HEAD_DIM], cosine, sine)[:, :, 0]
    key_rows = key_rows.astype(low_type)
    values = mixed[..., q_width + HEAD_DIM :].astype(low_type)
    soft_probs = jax.nn.softmax(masked_scores(queries, key_rows, allowed), axis=-1)
    low_probs = soft_probs.astype(low_type)
    attended = jnp.einsum("sgac,scd->sagd", low_probs, values, preferred_element_type=f32)
    attended = attended.reshape(8 * seq_len, q_width).astype(low_type)
    hidden = inputs + reduce_tokens(dot(attended, head_out).astype(low_type))

    hidden = after(hidden, *blocks[3:7])
    weight_gu = jnp.concatenate(
        [block[:units_own] for block in blocks]
        + [block[units_own : 2 * units_own] for block in blocks]
    )
    weight_down = jnp.concatenate([block[2 * units_own :] for block in blocks])
    unit_two, inverse_two = normalize(hidden)
    normed = gather_tokens((unit_two * gain_two).astype(low_type))[1].reshape(-1, width)
    rows = 8 * seq_len
    units = 8 * units_own
    pre = right_dot(normed, weight_gu)
    gate_pre, up_pre = pre[:, :units], pre[:, units:]
    grad_act = right_dot(cots, weight_down)
    sigmoid_gate = jax.nn.sigmoid(gate_pre)
    activated = (gate_pre * sigmoid_gate * up_pre).astype(low_type)
    grad_gate = grad_act * up_pre * sigmoid_gate * (1.0 + gate_pre * (1.0 - sigmoid_gate))
    grad_up = grad_act * gate_pre * sigmoid_gate
    grad_gu = jnp.concatenate([grad_gate.astype(low_type), grad_up.astype(low_type)], axis=1)
    grad_normed_two = reduce_tokens(dot(grad_gu, weight_gu).astype(low_type))
    term_gu = left_dot(grad_gu, normed).astype(low_type).reshape(2, 8, units_own, width)
    term_down = left_dot(activated, cots).astype(low_type).reshape(8, units_own, width)
    terms = [jnp.concatenate([term_gu[0, i], term_gu[1, i], term_down[i]]) for i in range(8)]
    sum_ffn = sum_replicas(reduce_weights(terms))
    sum_gate = jnp.stack([sum_ffn[:units_own].T, sum_ffn[units_own : 2 * units_own].T])
    sum_down = sum_ffn[2 * units_own :]
    layer_out = hidden + reduce_tokens(dot(activated, weight_down).astype(low_type))

    gain_terms = jnp.sum(grad_normed_two * unit_two, axis=0).astype(low_type).reshape(8, -1)
    gain_terms = swap(gain_terms, token_groups).astype(f32).sum(axis=0).astype(low_type)
    grad_hidden = grad_out + norm_back(grad_normed_two * gain_two, unit_two, inverse_two)

    branch = gather_tokens(grad_hidden.astype(low_type))[1].reshape(-1, width)
    term_out = left_dot(attended, branch).astype(low_type)
    grad_attended = right_dot(branch, head_out).astype(low_type)
    grad_attended = grad_attended.reshape(8, seq_len, GROUP, HEAD_DIM)
    grad_values = jnp.einsum(
        "sgac,sagd->scd", low_probs, grad_attended, preferred_element_type=f32
    )
    grad_probs = jnp.einsum("sagd,scd->sgac", grad_attended, values, preferred_element_type=f32)
    row_inner = jnp.sum(soft_probs * grad_probs, axis=-1, keepdims=True)
    grad_scores = (soft_probs * (grad_probs - row_inner) * HEAD_DIM ** (-0.5)).astype(low_type)
    grad_queries = jnp.einsum("sgac,scd->sagd", grad_scores, key_rows, preferred_element_type=f32)
    grad_keys = jnp.einsum("sgac,sagd->scd", grad_scores, queries, preferred_element_type=f32)
    grad_queries = rotate(grad_queries, cosine, -sine).reshape(8, seq_len, q_width)
    grad_keys = rotate(grad_keys[:, :, None], cosine, -sine)[:, :, 0]
    grad_mixed = jnp.concatenate([grad_queries, grad_keys, grad_values], axis=-1)
    grad_mixed = grad_mixed.reshape(rows, group_width).astype(low_type)
    grad_unit_one = reduce_tokens(right_dot(grad_mixed, head_in).astype(low_type))
    input_grad = grad_hidden + norm_back(grad_unit_one, unit_one, inverse_one)
    term_in = left_dot(units_one, grad_mixed).astype(low_type)

    gain_tiles = jnp.pad(
        gain_terms.reshape(8, 1, own_rows), ((0, 0), (0, 15), (0, width - own_rows))
    )
    out_tiles = jnp.concatenate([term_out.reshape(8, own_rows, width), gain_tiles], axis=1)
    sum_tile = send(reduce_small(out_tiles, x).astype(low_type), go_turn).astype(f32)
    sum_out, sum_gain_two = sum_tile[:own_rows], sum_tile[own_rows, :own_rows]
    chunk = reduce_small(term_in.reshape(8, 8 * own_rows, group_width), x).astype(low_type)
    groups = swap(chunk.reshape(8, own_rows, group_width), token_groups).transpose(1, 0, 2)
    sum_unit = jnp.concatenate(
        [
            groups[:, :, :q_width].reshape(own_rows, query_width),
            groups[:, :, q_width : q_width + HEAD_DIM].reshape(own_rows, kv_width),
            groups[:, :, q_width + HEAD_DIM :].reshape(own_rows, kv_width),
        ],
        axis=1,
    ).astype(f32)
    sum_in = sum_unit * gain_rows
    sum_gains = jnp.stack([jnp.sum(sum_unit * low_in, axis=1), sum_gain_two])

    new_in, moment_in, square_in = adam_update(
        project_in, sum_in, first_in, second_in, rate_matrix, decay_matrix
    )
    new_out, moment_out, square_out = adam_update(
        project_out, sum_out, first_out, second_out, rate_matrix, decay_matrix
    )
    new_gate, moment_gate, square_gate = adam_update(
        gate_up, sum_gate, first_gate, second_gate, rate_matrix, decay_matrix
    )
    new_down, moment_down, square_down = adam_update(
        down_weight, sum_down, first_down, second_down, rate_matrix, decay_matrix
    )
    new_gains, moment_gains, square_gains = adam_update(
        norm_gains, sum_gains, first_gains, second_gains, rate_gain, 0.0
    )
    return (
        layer_out,
        input_grad,
        new_in,
        new_out,
        new_gate,
        new_down,
        new_gains,
        moment_in,
        moment_out,
        moment_gate,
        moment_down,
        moment_gains,
        square_in,
        square_out,
        square_gate,
        square_down,
        square_gains,
    )


def solution(mesh):
    tokens_split = P(EVERY, None)
    weights = (P("shard", None), P("shard", None), P(None, None, "shard"), P("shard", None), P(None, "shard"))
    in_specs = (tokens_split,) * 3 + weights * 3
    out_specs = (tokens_split,) * 2 + weights * 3
    return jax.shard_map(local, mesh=mesh, in_specs=in_specs, out_specs=out_specs, check_vma=False)
```
